32 devices in a mesh: groups: 2 (over y), cache: 4 (over z), tensor: 4 (over x, core).
Axes of the slice: x: 2, y: 2, z: 4, core: 2. Of those that a mesh axis runs over, the one named last changes fastest.
Arguments:
- question_q: bfloat16 [16, 128, 8192], P(('groups', 'cache'), None, 'tensor'), parts along dimension 0, may hold values from -16 to 16
- question_kv: bfloat16 [16, 128, 8, 256], P(('groups', 'cache'), None, 'tensor'), parts along dimension 0, may hold values from -16 to 16
- passage_kv: bfloat16 [128, 8, 512, 256], P(('groups', 'cache'), 'tensor'), parts along dimension 0, may hold values from -6 to 6
- passage_ids: int32 [16, 8], P(('groups', 'cache')), parts along dimension 0, may hold values from 0 to 63, as said below
- passage_home: int32 [128], P('groups'), parts along dimension 0, may hold values from 0 to 63, as said below
- passage_offsets: int32 [16, 8], P(('groups', 'cache')), parts along dimension 0, may hold values from 0 to 3584, as said below
- out_weight: bfloat16 [8192, 8192], P('tensor', 'cache'), may hold values from -0.75 to 0.75
Outputs:
- mixed: bfloat16 [16, 128, 8192], P(('groups', 'cache'), None, 'tensor'), parts along dimension 0
The draws below stay inside these ranges and needn't reach their ends.
There are 2 independent parts, one for each index of `groups`. The reference program is written for one: setup_inputs(seed, part) draws one part's arguments, and reference() takes and returns one part's arrays. A program takes and returns all parts, laid end to end along the dimension named above; an argument that names none is the same for every part. Nothing has to cross between parts.
Inputs may be any that keep to these rules, and one draw needn't show every extreme that they name: `passage_ids`: the 16 ids of the requests of one cache index are distinct; at most 8 of them have their passage_home row on one cache index's shard of passage_kv, and one shard holds 8 of them for every cache index. A permutation: passage n is row passage_home[n] of passage_kv. `passage_offsets`: each row is 512 times a permutation of 0 to 7.
All inputs are finite; a program needn't handle non-finite values.
Results may differ from the reference program's by a relative error of at most 0.013.
Values may be sent and summed in bfloat16 or wider, within the bound.
A program may use at most 256 MiB of HBM per device.

```python
import math
import jax
import jax.numpy as jnp
from jax import lax

D = 8192
HEADS = 64
KVH = 8
HD = 128
PL = 512
QLEN = 128
NP = 8
REQ_DEV = 2
PASS_DEV = 16
REQUESTS = 8
PASSAGES = 64
HEAD_BLOCK = 16
N_CACHE = 4
N_TENSOR = 4


def passage_plan(key):
    home_rows = jax.random.permutation(jax.random.fold_in(key, 11), PASSAGES).astype(jnp.int32)
    hot_owner = jax.random.randint(jax.random.fold_in(key, 12), (), 0, N_CACHE)
    pick_count = REQ_DEV * NP
    capacity = min(pick_count, max(2, (2 * pick_count + N_CACHE - 1) // N_CACHE))
    local_score = jax.random.randint(jax.random.fold_in(key, 13), (N_CACHE, N_CACHE, PASS_DEV), 0, PASS_DEV)
    local_score = (local_score + jnp.arange(PASS_DEV)) * PASS_DEV + jnp.arange(PASS_DEV)
    local_order = jnp.argsort(local_score, axis=-1, stable=True)[..., :capacity].astype(jnp.int32)
    priority = jax.random.randint(jax.random.fold_in(key, 14), (N_CACHE, N_CACHE, capacity), 0, 1 << 20)
    priority = priority * (N_CACHE * capacity) + jnp.arange(N_CACHE * capacity).reshape(N_CACHE, capacity)
    priority = jnp.where(jnp.arange(N_CACHE)[None, :, None] == hot_owner, -1, priority)
    chosen = jnp.argsort(priority.reshape(N_CACHE, -1), axis=1, stable=True)[:, :pick_count].astype(jnp.int32)
    owner_index = chosen // capacity
    local_index = jnp.take_along_axis(local_order.reshape(N_CACHE, -1), chosen, axis=1)
    row_index = owner_index * PASS_DEV + local_index
    shuffle = jax.random.randint(jax.random.fold_in(key, 15), (N_CACHE, pick_count), 0, 1 << 20)
    shuffle_order = jnp.argsort(shuffle * pick_count + jnp.arange(pick_count), axis=1, stable=True)
    row_index = jnp.take_along_axis(row_index, shuffle_order, axis=1)
    inverse_home = jnp.argsort(home_rows, stable=True).astype(jnp.int32)
    passage_list = inverse_home[row_index].reshape(REQUESTS, NP).astype(jnp.int32)
    return (home_rows, passage_list)


def draw_passage_ids(key, part):
    return passage_plan(key)[1]


def draw_passage_home(key, part):
    return passage_plan(key)[0]


def draw_passage_offsets(key, part):
    key = jax.random.fold_in(key, 3)
    local_score = jax.random.randint(key, (REQUESTS, NP), 0, 1 << 16) * NP + jnp.arange(NP)
    return (jnp.argsort(local_score, axis=1, stable=True) * PL).astype(jnp.int32)


def draw_question_q(key, part):
    key = jax.random.fold_in(key, 5)
    sample = jnp.clip(2.0 * jax.random.normal(key, (REQUESTS, QLEN, HEADS, HD), jnp.float32), -12.0, 12.0)
    return sample.reshape(REQUESTS, QLEN, HEADS * HD).astype(jnp.bfloat16)


def draw_question_kv(key, part):
    key = jax.random.fold_in(key, 7)
    sample = jnp.clip(jax.random.normal(key, (REQUESTS, QLEN, KVH, 2 * HD), jnp.float32), -6.0, 6.0)
    return sample.astype(jnp.bfloat16)


def strengthened(values, own_key, source, target, blocks, factor):
    owner, partner = [(jnp.arange(values.shape[dim]) // (values.shape[dim] // blocks)).reshape([-1 if axis == dim else 1 for axis in range(values.ndim)]) for dim in (source, target)]
    chosen = jax.random.permutation(own_key, blocks)[partner]
    strong = (owner == chosen) | (owner == (partner + blocks // 2) % blocks)
    return jnp.where(strong, factor * values, values)


def shard_levels(rng, shape, cuts, least, top_value):
    loudness = 1.0
    for axis_at, parts in cuts:
        draws = jax.random.uniform(jax.random.fold_in(jax.random.fold_in(rng, 6), axis_at), (parts,), jnp.float32, least / len(cuts), top_value / len(cuts))
        loudness = loudness * jnp.repeat(jnp.exp(draws), shape[axis_at] // parts).reshape((-1,) + (1,) * (len(shape) - 1 - axis_at))
    return loudness


def noise(own_key, extent, deviation, most, split=(), kind=jnp.bfloat16):
    array = jax.random.normal(own_key, extent, jnp.float32) * deviation
    if len(split) > 0:
        array = shard_levels(own_key, extent, split, -0.22, 0.18) * array
    return jnp.clip(array, min=-most, max=most).astype(kind)


def noise_with(key, shape, deviation, reach, split, heavy, held_as=jnp.bfloat16):
    array = deviation * jax.random.normal(key, shape, jnp.float32)
    if split:
        array = array * shard_levels(key, shape, split, -0.22, 0.18)
    return jnp.clip(strengthened(array, jax.random.fold_in(key, 3), *heavy), -reach, reach).astype(held_as)


def setup_inputs(seed: int = 0, part: int = 0) -> dict:
    streams_of = jax.random.split(jax.random.key(seed), 8)
    part_keys = jax.random.split(jax.random.fold_in(streams_of[7], part), 8)
    return {
        "question_q": draw_question_q(jax.random.fold_in(jax.random.fold_in(streams_of[7], part), 71), part),
        "question_kv": draw_question_kv(jax.random.fold_in(jax.random.fold_in(streams_of[7], part), 71), part),
        "passage_kv": noise(part_keys[2], (PASSAGES, KVH, PL, 2 * HD), 1.0, 6.0, ((0, 4), (1, 4))),
        "passage_ids": draw_passage_ids(jax.random.fold_in(jax.random.fold_in(streams_of[7], part), 71), part),
        "passage_home": draw_passage_home(jax.random.fold_in(jax.random.fold_in(streams_of[7], part), 71), part),
        "passage_offsets": draw_passage_offsets(jax.random.fold_in(jax.random.fold_in(streams_of[7], part), 71), part),
        "out_weight": noise_with(streams_of[6], (HEADS * HD, D), HD ** -0.5, 0.75, ((0, 4), (1, 4)), (0, 1, 4, 2.0)),
    }


def frequencies(head_width):
    pair_index = jnp.arange(head_width // 2, dtype=jnp.float32)
    inverse = jnp.power(jnp.float32(500000.0), -2.0 * pair_index / head_width)
    wavelength = 2.0 * math.pi / inverse
    smooth = (8192.0 / wavelength - 1.0) / 3.0
    blended = (1.0 - smooth) * inverse / 8.0 + smooth * inverse
    return jnp.where(wavelength < 2048.0, inverse, jnp.where(wavelength > 8192.0, inverse / 8.0, blended))

def rotate(values, angles):
    half_width = values.shape[-1] // 2
    lower_half = values[..., :half_width]
    upper_half = values[..., half_width:]
    cosine = jnp.cos(angles)
    sine_values = jnp.sin(angles)
    return jnp.concatenate([lower_half * cosine - upper_half * sine_values, upper_half * cosine + lower_half * sine_values], axis=-1)

def attend(query_rows, own_pairs, passages, offsets, inverse):
    head_width = passages.shape[-1] // 2
    length = query_rows.shape[0]
    groups = own_pairs.shape[1]
    passage_count = passages.shape[0]
    span_tokens = passages.shape[2]
    positions = (passage_count * span_tokens + jnp.arange(length)).astype(jnp.float32)
    query_angles = positions[:, None] * inverse[None, :]
    queries = rotate(query_rows.reshape(length, groups, -1, head_width).astype(jnp.float32), query_angles[:, None, None, :]).astype(jnp.bfloat16)
    own_keys = rotate(own_pairs[..., :head_width].astype(jnp.float32), query_angles[:, None, :]).astype(jnp.bfloat16)
    own_values = own_pairs[..., head_width:]
    far_angles = offsets.astype(jnp.float32)[:, None] * inverse[None, :]
    far_keys = rotate(passages[..., :head_width].astype(jnp.float32), far_angles[:, None, None, :]).astype(jnp.bfloat16)
    far_values = passages[..., head_width:]
    score_scale = 1.0 / math.sqrt(head_width)
    heads_per = queries.shape[2]
    far_scores = jnp.einsum('tghd,ngpd->ghtnp', queries.astype(jnp.float32), far_keys.astype(jnp.float32))
    far_scores = far_scores.reshape(groups, heads_per, length, passage_count * span_tokens) * score_scale
    own_scores = jnp.einsum('tghd,sgd->ghts', queries.astype(jnp.float32), own_keys.astype(jnp.float32)) * score_scale
    causal = jnp.arange(length)[:, None] >= jnp.arange(length)[None, :]
    own_scores = jnp.where(causal, own_scores, -jnp.inf)
    scores = jnp.concatenate([far_scores, own_scores], axis=-1)
    row_top = lax.optimization_barrier(jnp.max(scores, axis=-1, keepdims=True))
    exponent = jnp.exp(scores - row_top)
    weights = (exponent / lax.optimization_barrier(jnp.sum(exponent, axis=-1, keepdims=True))).astype(jnp.bfloat16)
    far_weights = weights[..., :passage_count * span_tokens].reshape(groups, heads_per, length, passage_count, span_tokens)
    own_weights = weights[..., passage_count * span_tokens:]
    result = jnp.einsum('ghtnp,ngpd->tghd', far_weights.astype(jnp.float32), far_values.astype(jnp.float32))
    result = result + jnp.einsum('ghts,sgd->tghd', own_weights.astype(jnp.float32), own_values.astype(jnp.float32))
    return result.astype(jnp.bfloat16).reshape(length, -1)

def reference(question_q, question_kv, passage_kv, passage_ids, passage_home, passage_offsets, out_weight):
    inverse = frequencies(HD)
    passage_rows = passage_home[passage_ids]

    def one_request(request_items):
        query_rows, own_pairs, rows_here, offsets = request_items
        passages = jnp.take(passage_kv, rows_here, axis=0)
        return attend(query_rows, own_pairs, passages, offsets, inverse)
    attended = lax.map(one_request, (question_q, question_kv, passage_rows, passage_offsets))
    flat_rows = attended.reshape(REQUESTS * QLEN, N_TENSOR, HEAD_BLOCK * HD)
    blocks = out_weight.reshape(N_TENSOR, HEAD_BLOCK * HD, D)
    running = jnp.zeros((REQUESTS * QLEN, D), jnp.float32)
    for block_index in range(N_TENSOR):
        partial_value = jnp.dot(flat_rows[:, block_index], blocks[block_index], preferred_element_type=jnp.float32)
        partial_value = lax.optimization_barrier(partial_value.astype(jnp.bfloat16))
        running = running + partial_value.astype(jnp.float32)
    return running.astype(jnp.bfloat16).reshape(REQUESTS, QLEN, D)
```

```python
import functools
import math

import jax
import jax.numpy as jnp
from jax import lax
from jax.experimental import pallas as pl
from jax.experimental.pallas import tpu as pltpu
from jax.sharding import PartitionSpec as P

LOW = -1e30


def frequencies(head_width):
    pair_index = jnp.arange(head_width // 2, dtype=jnp.float32)
    inverse = jnp.power(jnp.float32(500000.0), -2.0 * pair_index / head_width)
    wavelength = 2.0 * math.pi / inverse
    smooth = (8192.0 / wavelength - 1.0) / 3.0
    blended = (1.0 - smooth) * inverse / 8.0 + smooth * inverse
    return jnp.where(
        wavelength < 2048.0, inverse, jnp.where(wavelength > 8192.0, inverse / 8.0, blended)
    )


def tables(positions, inverse):
    angles = positions.astype(jnp.float32)[:, None] * inverse[None, :]
    cosine, sine = jnp.cos(angles), jnp.sin(angles)
    return jnp.concatenate([cosine, cosine], 1), jnp.concatenate([-sine, sine], 1)


def turn(x, cosine, sine):
    return x * cosine + pltpu.roll(x, x.shape[1] // 2, 1) * sine


def fold(q, keys, values, masked, m_ref, acc_ref, rows, first):
    s = lax.dot_general(q, keys, (((1,), (1,)), ((), ())), preferred_element_type=jnp.float32)
    if masked is not None:
        s = jnp.where(masked, s, LOW)
    top = jnp.max(s, axis=1, keepdims=True)
    width = values.shape[1] // 2
    if first:
        new = jnp.broadcast_to(top, (s.shape[0], width))
    else:
        old = m_ref[rows, :]
        new = jnp.maximum(old, top)
    wide = new if s.shape[1] == width else jnp.concatenate([new] * (s.shape[1] // width), 1)
    p = jnp.exp2(s - wide).astype(jnp.bfloat16)
    pv = jnp.dot(p, values, preferred_element_type=jnp.float32)
    if not first:
        alpha = jnp.exp2(old - new)
        pv = acc_ref[rows, :] * jnp.concatenate([alpha, alpha], 1) + pv
    acc_ref[rows, :] = pv
    m_ref[rows, :] = new


def attend_kernel(
    listed, scale, me_ref, ids, home, q, kv, own, cq, sq, cf, sf, o, lse, qs, acc, m
):
    request = pl.program_id(0)
    stored, groups, span, both = kv.shape
    width = both // 2
    length = q.shape[1]
    heads = q.shape[2] // width
    per = heads // groups
    step = min(2, per)
    mine = me_ref[0]
    here = own.shape[0]
    ones = jnp.ones((span, width), jnp.bfloat16)
    for h in range(heads):
        x = q[0, :, h * width : (h + 1) * width].astype(jnp.float32)
        qs[h * length : (h + 1) * length, :] = (
            turn(x, cq[...], sq[...]) * scale
        ).astype(jnp.bfloat16)
    chunk = step * length

    @pl.when(request // here == mine)
    def _():
        r = request - mine * here
        at = lax.broadcasted_iota(jnp.int32, (chunk, length), 0) % length
        causal = at >= lax.broadcasted_iota(jnp.int32, (chunk, length), 1)
        for g in range(groups):
            pair = own[r, g]
            keys = turn(pair[:, :width].astype(jnp.float32), cq[...], sq[...])
            keys = keys.astype(jnp.bfloat16)
            values = jnp.concatenate([pair[:, width:], ones[:length]], 1)
            for i in range(per // step):
                rows = pl.ds((g * per + i * step) * length, chunk)
                fold(qs[rows, :], keys, values, causal, m, acc, rows, True)

    @pl.when(request // here != mine)
    def _():
        m[...] = jnp.full_like(m, LOW)
        acc[...] = jnp.zeros_like(acc)

    def slot(j, carry):
        at = request * listed + j
        row = home[ids[at]]

        @pl.when(row // stored == mine)
        def _():
            local = row - mine * stored
            cosine, sine = cf[pl.ds(at, 1), :], sf[pl.ds(at, 1), :]
            for g in range(groups):
                pair = kv[local, g]
                keys = turn(pair[:, :width].astype(jnp.float32), cosine, sine)
                keys = keys.astype(jnp.bfloat16)
                values = jnp.concatenate([pair[:, width:], ones], 1)
                for i in range(per // step):
                    rows = pl.ds((g * per + i * step) * length, chunk)
                    fold(qs[rows, :], keys, values, None, m, acc, rows, False)

        return carry

    lax.fori_loop(0, listed, slot, 0)
    eye = lax.broadcasted_iota(jnp.int32, (length, width), 0) == lax.broadcasted_iota(
        jnp.int32, (length, width), 1
    )
    for h in range(heads):
        rows = pl.ds(h * length, length)
        total = acc[rows, width:]
        some = total > 0.0
        safe = jnp.where(some, total, 1.0)
        o[0, :, h * width : (h + 1) * width] = (acc[rows, :width] / safe).astype(jnp.bfloat16)
        level = jnp.where(some, m[rows, :] + jnp.log2(safe), LOW)
        lse[0, h : h + 1, :] = jnp.sum(jnp.where(eye, level, 0.0), axis=0, keepdims=True)


def attend(me, ids, home, q, kv, own, cq, sq, cf, sf):
    requests, length, span = q.shape
    groups, both = kv.shape[1], kv.shape[3]
    width = both // 2
    heads = span // width
    whole = lambda a: pl.BlockSpec(a.shape, lambda i: (0,) * a.ndim, pipeline_mode=pl.Buffered(1))
    smem = pl.BlockSpec(memory_space=pltpu.SMEM)
    return pl.pallas_call(
        functools.partial(
            attend_kernel, ids.shape[0] // requests, math.log2(math.e) / math.sqrt(width)
        ),
        grid=(requests,),
        in_specs=[
            smem,
            smem,
            smem,
            pl.BlockSpec((1, length, span), lambda i: (i, 0, 0)),
            whole(kv),
            whole(own),
            whole(cq),
            whole(sq),
            whole(cf),
            whole(sf),
        ],
        out_specs=[
            pl.BlockSpec((1, length, span), lambda i: (i, 0, 0)),
            pl.BlockSpec((1, heads, length), lambda i: (i, 0, 0)),
        ],
        out_shape=[
            jax.ShapeDtypeStruct((requests, length, span), jnp.bfloat16),
            jax.ShapeDtypeStruct((requests, heads, length), jnp.float32),
        ],
        scratch_shapes=[
            pltpu.VMEM((heads * length, width), jnp.bfloat16),
            pltpu.VMEM((heads * length, 2 * width), jnp.float32),
            pltpu.VMEM((heads * length, width), jnp.float32),
        ],
        compiler_params=pltpu.CompilerParams(vmem_limit_bytes=40 * 1024 * 1024),
    )(me, ids, home, q, kv, own, cq, sq, cf, sf)


def merge_kernel(o, lse, out):
    count, _, heads, length = lse.shape
    width = o.shape[3] // heads
    levels = [lse[c, 0] for c in range(count)]
    top = functools.reduce(jnp.maximum, levels)
    shares = [jnp.exp2(level - top) for level in levels]
    total = functools.reduce(jnp.add, shares)
    shares = [share / total for share in shares]
    for h in range(heads):
        at = slice(h * width, (h + 1) * width)
        result = jnp.zeros((length, width), jnp.float32)
        for c in range(count):
            column = jnp.transpose(jnp.broadcast_to(shares[c][h : h + 1, :], (width, length)))
            result += o[c, 0, :, at].astype(jnp.float32) * column
        out[0, :, at] = result.astype(jnp.bfloat16)


def merge(o, lse):
    count, requests, length, span = o.shape
    heads = lse.shape[2]
    return pl.pallas_call(
        merge_kernel,
        grid=(requests,),
        in_specs=[
            pl.BlockSpec((count, 1, length, span), lambda i: (0, i, 0, 0)),
            pl.BlockSpec((count, 1, heads, length), lambda i: (0, i, 0, 0)),
        ],
        out_specs=pl.BlockSpec((1, length, span), lambda i: (i, 0, 0)),
        out_shape=jax.ShapeDtypeStruct((requests, length, span), jnp.bfloat16),
        compiler_params=pltpu.CompilerParams(vmem_limit_bytes=40 * 1024 * 1024),
    )(o, lse)


def local(
    question_q, question_kv, passage_kv, passage_ids, passage_home, passage_offsets, out_weight
):
    caches, tensors = lax.axis_size("cache"), lax.axis_size("tensor")
    me_cache, me_tensor = lax.axis_index("cache"), lax.axis_index("tensor")
    here, length, span = question_q.shape
    width = passage_kv.shape[-1] // 2
    listed = passage_ids.shape[1]
    inverse = frequencies(width)
    lists = lax.all_gather(
        jnp.stack([passage_ids, passage_offsets]), "cache", axis=1, tiled=True
    )
    ids, offsets = lists[0].reshape(-1), lists[1].reshape(-1)
    q_all = lax.all_gather(question_q, "cache", axis=0, tiled=True)
    cq, sq = tables(listed * passage_kv.shape[2] + jnp.arange(length), inverse)
    cf, sf = tables(offsets, inverse)
    own = jnp.swapaxes(question_kv, 1, 2)
    o, lse = attend(
        me_cache.reshape(1).astype(jnp.int32), ids, passage_home, q_all, passage_kv, own,
        cq, sq, cf, sf,
    )
    o = lax.all_to_all(o, "cache", split_axis=0, concat_axis=0, tiled=True)
    lse = lax.all_to_all(lse, "cache", split_axis=0, concat_axis=0, tiled=True)
    attended = merge(
        o.reshape((caches, here, length, span)), lse.reshape((caches, here) + lse.shape[1:])
    )
    rows = lax.all_gather(attended.reshape(here * length, span), "cache", axis=0, tiled=True)
    partial = jnp.dot(rows, out_weight, preferred_element_type=jnp.float32)
    summed = lax.psum_scatter(
        partial.astype(jnp.bfloat16), "tensor", scatter_dimension=0, tiled=True
    )
    fan = caches // tensors
    tokens = here * length
    columns = out_weight.shape[1]
    blocks = summed.reshape(fan, tokens, columns)
    pieces = []
    for turn_at in range(fan):
        pairs = []
        for c in range(caches):
            for t in range(tensors):
                to = (t * fan + (turn_at + c % fan) % fan, c // fan)
                pairs.append((c * tensors + t, to[0] * tensors + to[1]))
        block = blocks[0]
        if fan > 1:
            block = lax.dynamic_index_in_dim(blocks, (turn_at + me_cache) % fan, 0, False)
        pieces.append(lax.ppermute(block, ("cache", "tensor"), pairs))
    if fan == 1:
        mixed = pieces[0]
    else:
        stacked = jnp.stack(pieces)
        order = (me_cache - jnp.arange(fan)) % fan
        mixed = jnp.take(stacked, order, axis=0)
        mixed = jnp.swapaxes(mixed, 0, 1).reshape(tokens, fan * columns)
    return mixed.reshape(here, length, -1)


def solution(mesh):
    in_specs = (
        P(("groups", "cache"), None, "tensor"),
        P(("groups", "cache"), None, "tensor", None),
        P(("groups", "cache"), "tensor", None, None),
        P(("groups", "cache"), None),
        P("groups"),
        P(("groups", "cache"), None),
        P("tensor", "cache"),
    )
    out_specs = P(("groups", "cache"), None, "tensor")
    return jax.shard_map(local, mesh=mesh, in_specs=in_specs, out_specs=out_specs, check_vma=False)
```

```python
import functools
import math

import jax
import jax.numpy as jnp
from jax import lax
from jax.experimental import pallas as pl
from jax.experimental.pallas import tpu as pltpu
from jax.sharding import PartitionSpec as P

LOW = -1e30
EXTRA = 16


def frequencies(head_width):
    pair_index = jnp.arange(head_width // 2, dtype=jnp.float32)
    inverse = jnp.power(jnp.float32(500000.0), -2.0 * pair_index / head_width)
    wavelength = 2.0 * math.pi / inverse
    smooth = (8192.0 / wavelength - 1.0) / 3.0
    blended = (1.0 - smooth) * inverse / 8.0 + smooth * inverse
    return jnp.where(
        wavelength < 2048.0, inverse, jnp.where(wavelength > 8192.0, inverse / 8.0, blended)
    )


def tables(positions, inverse):
    angles = positions.astype(jnp.float32)[:, None] * inverse[None, :]
    cosine, sine = jnp.cos(angles), jnp.sin(angles)
    return jnp.concatenate([cosine, cosine], 1), jnp.concatenate([-sine, sine], 1)


def turn(x, cosine, sine):
    return x * cosine + pltpu.roll(x, x.shape[1] // 2, 1) * sine


def fold(q, keys, values, masked, m_ref, acc_ref, rows, first):
    s = lax.dot_general(q, keys, (((1,), (1,)), ((), ())), preferred_element_type=jnp.float32)
    if masked is not None:
        s = jnp.where(masked, s, LOW)
    top = jnp.max(s, axis=1, keepdims=True)
    width = values.shape[1] // 2
    if first:
        new = jnp.broadcast_to(top, (s.shape[0], width))
    else:
        old = m_ref[rows, :]
        new = jnp.maximum(old, top)
    wide = new if s.shape[1] == width else jnp.concatenate([new] * (s.shape[1] // width), 1)
    p = jnp.exp2(s - wide).astype(jnp.bfloat16)
    pv = jnp.dot(p, values, preferred_element_type=jnp.float32)
    if not first:
        alpha = jnp.exp2(old - new)
        pv = acc_ref[rows, :] * jnp.concatenate([alpha, alpha], 1) + pv
    acc_ref[rows, :] = pv
    m_ref[rows, :] = new


def attend_kernel(
    listed, scale, me_ref, ids, home, q, kv, own, cq, sq, cf, sf, o, qs, acc, m
):
    request = pl.program_id(0)
    stored, groups, span, both = kv.shape
    width = both // 2
    length = own.shape[2]
    heads = q.shape[2] // width
    per = heads // groups
    step = min(2, per)
    mine = me_ref[0]
    here = own.shape[0]
    ones = jnp.ones((span, width), jnp.bfloat16)
    for h in range(heads):
        x = q[0, :length, h * width : (h + 1) * width].astype(jnp.float32)
        qs[h * length : (h + 1) * length, :] = (
            turn(x, cq[...], sq[...]) * scale
        ).astype(jnp.bfloat16)
    chunk = step * length

    @pl.when(request // here == mine)
    def _():
        r = request - mine * here
        at = lax.broadcasted_iota(jnp.int32, (chunk, length), 0) % length
        causal = at >= lax.broadcasted_iota(jnp.int32, (chunk, length), 1)
        for g in range(groups):
            pair = own[r, g]
            keys = turn(pair[:, :width].astype(jnp.float32), cq[...], sq[...])
            keys = keys.astype(jnp.bfloat16)
            values = jnp.concatenate([pair[:, width:], ones[:length]], 1)
            for i in range(per // step):
                rows = pl.ds((g * per + i * step) * length, chunk)
                fold(qs[rows, :], keys, values, causal, m, acc, rows, True)

    @pl.when(request // here != mine)
    def _():
        m[...] = jnp.full_like(m, LOW)
        acc[...] = jnp.zeros_like(acc)

    def slot(j, carry):
        at = request * listed + j
        row = home[ids[at]]

        @pl.when(row // stored == mine)
        def _():
            local = row - mine * stored
            cosine, sine = cf[pl.ds(at, 1), :], sf[pl.ds(at, 1), :]
            for g in range(groups):
                pair = kv[local, g]
                keys = turn(pair[:, :width].astype(jnp.float32), cosine, sine)
                keys = keys.astype(jnp.bfloat16)
                values = jnp.concatenate([pair[:, width:], ones], 1)
                for i in range(per // step):
                    rows = pl.ds((g * per + i * step) * length, chunk)
                    fold(qs[rows, :], keys, values, None, m, acc, rows, False)

        return carry

    lax.fori_loop(0, listed, slot, 0)
    eye = lax.broadcasted_iota(jnp.int32, (length, width), 0) == lax.broadcasted_iota(
        jnp.int32, (length, width), 1
    )
    for h in range(heads):
        rows = pl.ds(h * length, length)
        total = acc[rows, width:]
        some = total > 0.0
        safe = jnp.where(some, total, 1.0)
        at = slice(h * width, (h + 1) * width)
        o[0, :length, at] = (acc[rows, :width] / safe).astype(jnp.bfloat16)
        level = jnp.where(some, m[rows, :] + jnp.log2(safe), LOW)
        level = jnp.sum(jnp.where(eye, level, 0.0), axis=0, keepdims=True)
        high = level.astype(jnp.bfloat16).astype(jnp.float32)
        middle = (level - high).astype(jnp.bfloat16).astype(jnp.float32)
        low = level - high - middle
        line = lax.broadcasted_iota(jnp.int32, (EXTRA, width), 0)
        parts = jnp.where(line == 0, high, jnp.where(line == 1, middle, jnp.where(line == 2, low, 0.0)))
        o[0, length:, at] = parts.astype(jnp.bfloat16)


def attend(me, ids, home, q, kv, own, cq, sq, cf, sf):
    requests, rows, span = q.shape
    length = own.shape[2]
    width = kv.shape[3] // 2
    heads = span // width
    whole = lambda a: pl.BlockSpec(a.shape, lambda i: (0,) * a.ndim, pipeline_mode=pl.Buffered(1))
    smem = pl.BlockSpec(memory_space=pltpu.SMEM)
    return pl.pallas_call(
        functools.partial(
            attend_kernel, ids.shape[0] // requests, math.log2(math.e) / math.sqrt(width)
        ),
        grid=(requests,),
        in_specs=[
            smem,
            smem,
            smem,
            pl.BlockSpec((1, rows, span), lambda i: (i, 0, 0)),
            whole(kv),
            whole(own),
            whole(cq),
            whole(sq),
            whole(cf),
            whole(sf),
        ],
        out_specs=pl.BlockSpec((1, rows, span), lambda i: (i, 0, 0)),
        out_shape=jax.ShapeDtypeStruct((requests, rows, span), jnp.bfloat16),
        scratch_shapes=[
            pltpu.VMEM((heads * length, width), jnp.bfloat16),
            pltpu.VMEM((heads * length, 2 * width), jnp.float32),
            pltpu.VMEM((heads * length, width), jnp.float32),
        ],
        compiler_params=pltpu.CompilerParams(vmem_limit_bytes=40 * 1024 * 1024),
        cost_estimate=pl.CostEstimate(
            flops=requests * 4 * 4 * length * kv.shape[2] * span,
            bytes_accessed=2 * (kv.size + 2 * q.size),
            transcendentals=requests * 4 * heads * length * kv.shape[2],
        ),
    )(me, ids, home, q, kv, own, cq, sq, cf, sf)


def merge_kernel(*refs):
    out = refs[-1]
    parts = refs[:-1]
    length = out.shape[0]
    width = length
    heads = out.shape[1] // width
    for h in range(heads):
        at = slice(h * width, (h + 1) * width)
        levels = []
        for o in parts:
            tail = o[length:, at].astype(jnp.float32)
            levels.append(tail[0:1] + tail[1:2] + tail[2:3])
        top = functools.reduce(jnp.maximum, levels)
        shares = [jnp.exp2(level - top) for level in levels]
        total = functools.reduce(jnp.add, shares)
        result = jnp.zeros((length, width), jnp.float32)
        for o, share in zip(parts, shares):
            column = jnp.transpose(jnp.broadcast_to(share / total, (width, length)))
            result += o[:length, at].astype(jnp.float32) * column
        out[:, at] = result.astype(jnp.bfloat16)


def merge(parts, length):
    rows, span = parts[0].shape
    return pl.pallas_call(
        merge_kernel,
        out_shape=jax.ShapeDtypeStruct((length, span), jnp.bfloat16),
        compiler_params=pltpu.CompilerParams(vmem_limit_bytes=48 * 1024 * 1024),
    )(*parts)


def local(
    question_q, question_kv, passage_kv, passage_ids, passage_home, passage_offsets, out_weight
):
    caches, tensors = lax.axis_size("cache"), lax.axis_size("tensor")
    me_cache, me_tensor = lax.axis_index("cache"), lax.axis_index("tensor")
    here, length, span = question_q.shape
    width = passage_kv.shape[-1] // 2
    listed = passage_ids.shape[1]
    inverse = frequencies(width)
    cq, sq = tables(listed * passage_kv.shape[2] + jnp.arange(length), inverse)
    own = jnp.swapaxes(question_kv, 1, 2)
    me = me_cache.reshape(1).astype(jnp.int32)
    lists = jnp.stack([passage_ids, passage_offsets], 1).astype(jnp.bfloat16)
    lists = jnp.pad(lists, ((0, 0), (0, EXTRA - 2), (0, span - listed)))
    sent = jnp.concatenate([question_q, lists], 1)

    gathered = [lax.all_gather(sent[r], "cache", axis=0) for r in range(here)]
    exchanged, pieces = [], []
    for r in range(here):
        q = gathered[r]
        lists_r = q[:, length : length + 2, :listed].astype(jnp.int32)
        ids, offsets = lists_r[:, 0].reshape(-1), lists_r[:, 1].reshape(-1)
        cf, sf = tables(offsets, inverse)
        o = attend(me, ids, passage_home, q, passage_kv, own[r : r + 1], cq, sq, cf, sf)
        if exchanged:
            exchanged[-1], o = lax.optimization_barrier((exchanged[-1], o))
        parts = [lax.dynamic_index_in_dim(o, me_cache, 0, False)]
        for k in range(1, caches):
            block = lax.dynamic_index_in_dim(o, (me_cache + k) % caches, 0, False)
            parts.append(
                lax.ppermute(block, "cache", [(c, (c + k) % caches) for c in range(caches)])
            )
        exchanged.append(parts)
    for parts in exchanged:
        attended = merge(parts, length)
        rows = lax.all_gather(attended, "cache", axis=0, tiled=True)
        partial = jnp.dot(rows, out_weight, preferred_element_type=jnp.float32)
        summed = lax.psum_scatter(
            partial.astype(jnp.bfloat16), "tensor", scatter_dimension=0, tiled=True
        )
        pieces.append(deliver(summed, caches, tensors, me_cache, length))
    return jnp.stack(pieces)


def deliver(summed, caches, tensors, me_cache, tokens):
    fan = caches // tensors
    columns = summed.shape[1]
    blocks = summed.reshape(fan, tokens, columns)
    pieces = []
    for turn_at in range(fan):
        pairs = []
        for c in range(caches):
            for t in range(tensors):
                to = (t * fan + (turn_at + c % fan) % fan, c // fan)
                pairs.append((c * tensors + t, to[0] * tensors + to[1]))
        block = blocks[0]
        if fan > 1:
            block = lax.dynamic_index_in_dim(blocks, (turn_at + me_cache) % fan, 0, False)
        pieces.append(lax.ppermute(block, ("cache", "tensor"), pairs))
    if fan == 1:
        return pieces[0]
    order = (me_cache - jnp.arange(fan)) % fan
    mixed = jnp.take(jnp.stack(pieces), order, axis=0)
    return jnp.swapaxes(mixed, 0, 1).reshape(tokens, fan * columns)


def solution(mesh):
    in_specs = (
        P(("groups", "cache"), None, "tensor"),
        P(("groups", "cache"), None, "tensor", None),
        P(("groups", "cache"), "tensor", None, None),
        P(("groups", "cache"), None),
        P("groups"),
        P(("groups", "cache"), None),
        P("tensor", "cache"),
    )
    out_specs = P(("groups", "cache"), None, "tensor")
    return jax.shard_map(local, mesh=mesh, in_specs=in_specs, out_specs=out_specs, check_vma=False)
```

```python
import functools
import math

import jax
import jax.numpy as jnp
from jax import lax
from jax.experimental import pallas as pl
from jax.experimental.pallas import tpu as pltpu
from jax.sharding import PartitionSpec as P

LOW = -1e30
EXTRA = 16


def frequencies(head_width):
    pair_index = jnp.arange(head_width // 2, dtype=jnp.float32)
    inverse = jnp.power(jnp.float32(500000.0), -2.0 * pair_index / head_width)
    wavelength = 2.0 * math.pi / inverse
    smooth = (8192.0 / wavelength - 1.0) / 3.0
    blended = (1.0 - smooth) * inverse / 8.0 + smooth * inverse
    return jnp.where(
        wavelength < 2048.0, inverse, jnp.where(wavelength > 8192.0, inverse / 8.0, blended)
    )


def tables(positions, inverse):
    angles = positions.astype(jnp.float32)[:, None] * inverse[None, :]
    cosine, sine = jnp.cos(angles), jnp.sin(angles)
    return jnp.concatenate([cosine, cosine], 1), jnp.concatenate([-sine, sine], 1)


def turn(x, cosine, sine):
    return x * cosine + pltpu.roll(x, x.shape[1] // 2, 1) * sine


def fold(q, keys, values, masked, m_ref, acc_ref, rows, first):
    s = lax.dot_general(q, keys, (((1,), (1,)), ((), ())), preferred_element_type=jnp.float32)
    if masked is not None:
        s = jnp.where(masked, s, LOW)
    top = jnp.max(s, axis=1, keepdims=True)
    width = values.shape[1] // 2
    if first:
        new = jnp.broadcast_to(top, (s.shape[0], width))
    else:
        old = m_ref[rows, :]
        new = jnp.maximum(old, top)
    wide = new if s.shape[1] == width else jnp.concatenate([new] * (s.shape[1] // width), 1)
    p = jnp.exp2(s - wide).astype(jnp.bfloat16)
    pv = jnp.dot(p, values, preferred_element_type=jnp.float32)
    if not first:
        alpha = jnp.exp2(old - new)
        pv = acc_ref[rows, :] * jnp.concatenate([alpha, alpha], 1) + pv
    acc_ref[rows, :] = pv
    m_ref[rows, :] = new


def attend_kernel(
    listed, scale, me_ref, ids, home, q, kv, own, cq, sq, cf, sf, o, qs, acc, m
):
    request = pl.program_id(0)
    stored, groups, span, both = kv.shape
    width = both // 2
    length = own.shape[2]
    heads = q.shape[2] // width
    per = heads // groups
    step = min(2, per)
    mine = me_ref[0]
    here = own.shape[0]
    ones = jnp.ones((span, width), jnp.bfloat16)
    for h in range(heads):
        x = q[0, :length, h * width : (h + 1) * width].astype(jnp.float32)
        qs[h * length : (h + 1) * length, :] = (
            turn(x, cq[...], sq[...]) * scale
        ).astype(jnp.bfloat16)
    chunk = step * length

    @pl.when(request // here == mine)
    def _():
        r = request - mine * here
        at = lax.broadcasted_iota(jnp.int32, (chunk, length), 0) % length
        causal = at >= lax.broadcasted_iota(jnp.int32, (chunk, length), 1)
        for g in range(groups):
            pair = own[r, g]
            keys = turn(pair[:, :width].astype(jnp.float32), cq[...], sq[...])
            keys = keys.astype(jnp.bfloat16)
            values = jnp.concatenate([pair[:, width:], ones[:length]], 1)
            for i in range(per // step):
                rows = pl.ds((g * per + i * step) * length, chunk)
                fold(qs[rows, :], keys, values, causal, m, acc, rows, True)

    @pl.when(request // here != mine)
    def _():
        m[...] = jnp.full_like(m, LOW)
        acc[...] = jnp.zeros_like(acc)

    def slot(j, carry):
        at = request * listed + j
        row = home[ids[at]]

        @pl.when(row // stored == mine)
        def _():
            local = row - mine * stored
            cosine, sine = cf[pl.ds(at, 1), :], sf[pl.ds(at, 1), :]
            for g in range(groups):
                pair = kv[local, g]
                keys = turn(pair[:, :width].astype(jnp.float32), cosine, sine)
                keys = keys.astype(jnp.bfloat16)
                values = jnp.concatenate([pair[:, width:], ones], 1)
                for i in range(per // step):
                    rows = pl.ds((g * per + i * step) * length, chunk)
                    fold(qs[rows, :], keys, values, None, m, acc, rows, False)

        return carry

    lax.fori_loop(0, listed, slot, 0)
    eye = lax.broadcasted_iota(jnp.int32, (length, width), 0) == lax.broadcasted_iota(
        jnp.int32, (length, width), 1
    )
    for h in range(heads):
        rows = pl.ds(h * length, length)
        total = acc[rows, width:]
        some = total > 0.0
        safe = jnp.where(some, total, 1.0)
        at = slice(h * width, (h + 1) * width)
        o[0, :length, at] = (acc[rows, :width] / safe).astype(jnp.bfloat16)
        level = jnp.where(some, m[rows, :] + jnp.log2(safe), LOW)
        level = jnp.sum(jnp.where(eye, level, 0.0), axis=0, keepdims=True)
        high = level.astype(jnp.bfloat16).astype(jnp.float32)
        middle = (level - high).astype(jnp.bfloat16).astype(jnp.float32)
        low = level - high - middle
        line = lax.broadcasted_iota(jnp.int32, (EXTRA, width), 0)
        parts = jnp.where(line == 0, high, jnp.where(line == 1, middle, jnp.where(line == 2, low, 0.0)))
        o[0, length:, at] = parts.astype(jnp.bfloat16)


def attend(me, ids, home, q, kv, own, cq, sq, cf, sf):
    requests, rows, span = q.shape
    length = own.shape[2]
    width = kv.shape[3] // 2
    heads = span // width
    whole = lambda a: pl.BlockSpec(a.shape, lambda i: (0,) * a.ndim, pipeline_mode=pl.Buffered(1))
    smem = pl.BlockSpec(memory_space=pltpu.SMEM)
    return pl.pallas_call(
        functools.partial(
            attend_kernel, ids.shape[0] // requests, math.log2(math.e) / math.sqrt(width)
        ),
        grid=(requests,),
        in_specs=[
            smem,
            smem,
            smem,
            pl.BlockSpec((1, rows, span), lambda i: (i, 0, 0)),
            whole(kv),
            whole(own),
            whole(cq),
            whole(sq),
            whole(cf),
            whole(sf),
        ],
        out_specs=pl.BlockSpec((1, rows, span), lambda i: (i, 0, 0)),
        out_shape=jax.ShapeDtypeStruct((requests, rows, span), jnp.bfloat16),
        scratch_shapes=[
            pltpu.VMEM((heads * length, width), jnp.bfloat16),
            pltpu.VMEM((heads * length, 2 * width), jnp.float32),
            pltpu.VMEM((heads * length, width), jnp.float32),
        ],
        compiler_params=pltpu.CompilerParams(vmem_limit_bytes=40 * 1024 * 1024),
        cost_estimate=pl.CostEstimate(
            flops=requests * 4 * 4 * length * kv.shape[2] * span,
            bytes_accessed=2 * (kv.size + 2 * q.size),
            transcendentals=requests * 4 * heads * length * kv.shape[2],
        ),
    )(me, ids, home, q, kv, own, cq, sq, cf, sf)


def merge_kernel(o, out):
    count = o.shape[0]
    length = out.shape[1]
    width = length
    heads = out.shape[2] // width
    for h in range(heads):
        at = slice(h * width, (h + 1) * width)
        levels = []
        for c in range(count):
            tail = o[c, 0, length:, at].astype(jnp.float32)
            levels.append(tail[0:1] + tail[1:2] + tail[2:3])
        top = functools.reduce(jnp.maximum, levels)
        shares = [jnp.exp2(level - top) for level in levels]
        total = functools.reduce(jnp.add, shares)
        result = jnp.zeros((length, width), jnp.float32)
        for c in range(count):
            column = jnp.transpose(jnp.broadcast_to(shares[c] / total, (width, length)))
            result += o[c, 0, :length, at].astype(jnp.float32) * column
        out[0, :, at] = result.astype(jnp.bfloat16)


def merge(o, length):
    count, requests, rows, span = o.shape
    return pl.pallas_call(
        merge_kernel,
        grid=(requests,),
        in_specs=[pl.BlockSpec((count, 1, rows, span), lambda i: (0, i, 0, 0))],
        out_specs=pl.BlockSpec((1, length, span), lambda i: (i, 0, 0)),
        out_shape=jax.ShapeDtypeStruct((requests, length, span), jnp.bfloat16),
        compiler_params=pltpu.CompilerParams(vmem_limit_bytes=40 * 1024 * 1024),
    )(o)


def local(
    question_q, question_kv, passage_kv, passage_ids, passage_home, passage_offsets, out_weight
):
    caches, tensors = lax.axis_size("cache"), lax.axis_size("tensor")
    me_cache, me_tensor = lax.axis_index("cache"), lax.axis_index("tensor")
    here, length, span = question_q.shape
    width = passage_kv.shape[-1] // 2
    listed = passage_ids.shape[1]
    inverse = frequencies(width)
    cq, sq = tables(listed * passage_kv.shape[2] + jnp.arange(length), inverse)
    own = jnp.swapaxes(question_kv, 1, 2)
    me = me_cache.reshape(1).astype(jnp.int32)
    lists = jnp.stack([passage_ids, passage_offsets], 1).astype(jnp.bfloat16)
    lists = jnp.pad(lists, ((0, 0), (0, EXTRA - 2), (0, span - listed)))
    sent = jnp.concatenate([question_q, lists], 1)

    q = lax.all_gather(sent, "cache", axis=0, tiled=True)
    lists = q[:, length : length + 2, :listed].astype(jnp.int32)
    ids, offsets = lists[:, 0].reshape(-1), lists[:, 1].reshape(-1)
    cf, sf = tables(offsets, inverse)
    o = attend(me, ids, passage_home, q, passage_kv, own, cq, sq, cf, sf)
    o = lax.all_to_all(o, "cache", split_axis=0, concat_axis=0, tiled=True)
    attended = merge(o.reshape((caches, here) + o.shape[1:]), length)
    tokens = here * length
    rows = lax.all_gather(attended.reshape(tokens, span), "cache", axis=0, tiled=True)
    parts = 2
    columns = out_weight.shape[1] // parts
    pieces = []
    for i in range(parts):
        partial = jnp.dot(
            rows,
            out_weight[:, i * columns : (i + 1) * columns],
            preferred_element_type=jnp.float32,
        )
        summed = lax.psum_scatter(
            partial.astype(jnp.bfloat16), "tensor", scatter_dimension=0, tiled=True
        )
        pieces.append(deliver(summed, caches, tensors, me_cache, tokens))
    mixed = jnp.stack(pieces, 2)
    return mixed.reshape(here, length, -1)


def deliver(summed, caches, tensors, me_cache, tokens):
    fan = caches // tensors
    columns = summed.shape[1]
    blocks = summed.reshape(fan, tokens, columns)
    pieces = []
    for turn_at in range(fan):
        pairs = []
        for c in range(caches):
            for t in range(tensors):
                to = (t * fan + (turn_at + c % fan) % fan, c // fan)
                pairs.append((c * tensors + t, to[0] * tensors + to[1]))
        block = blocks[0]
        if fan > 1:
            block = lax.dynamic_index_in_dim(blocks, (turn_at + me_cache) % fan, 0, False)
        pieces.append(lax.ppermute(block, ("cache", "tensor"), pairs))
    if fan == 1:
        return pieces[0][:, None]
    order = (me_cache - jnp.arange(fan)) % fan
    return jnp.swapaxes(jnp.take(jnp.stack(pieces), order, axis=0), 0, 1)


def solution(mesh):
    in_specs = (
        P(("groups", "cache"), None, "tensor"),
        P(("groups", "cache"), None, "tensor", None),
        P(("groups", "cache"), "tensor", None, None),
        P(("groups", "cache"), None),
        P("groups"),
        P(("groups", "cache"), None),
        P("tensor", "cache"),
    )
    out_specs = P(("groups", "cache"), None, "tensor")
    return jax.shard_map(local, mesh=mesh, in_specs=in_specs, out_specs=out_specs, check_vma=False)
```

```python
import functools
import math

import jax
import jax.numpy as jnp
from jax import lax
from jax.experimental import pallas as pl
from jax.experimental.pallas import tpu as pltpu
from jax.sharding import PartitionSpec as P

LOW = -1e30


def frequencies(head_width):
    pair_index = jnp.arange(head_width // 2, dtype=jnp.float32)
    inverse = jnp.power(jnp.float32(500000.0), -2.0 * pair_index / head_width)
    wavelength = 2.0 * math.pi / inverse
    smooth = (8192.0 / wavelength - 1.0) / 3.0
    blended = (1.0 - smooth) * inverse / 8.0 + smooth * inverse
    return jnp.where(
        wavelength < 2048.0, inverse, jnp.where(wavelength > 8192.0, inverse / 8.0, blended)
    )


def tables(positions, inverse):
    angles = positions.astype(jnp.float32)[:, None] * inverse[None, :]
    cosine, sine = jnp.cos(angles), jnp.sin(angles)
    return jnp.concatenate([cosine, cosine], 1), jnp.concatenate([-sine, sine], 1)


def turn(x, cosine, sine):
    return x * cosine + pltpu.roll(x, x.shape[1] // 2, 1) * sine


def fold(q, keys, values, masked, m_ref, acc_ref, rows, first):
    s = lax.dot_general(q, keys, (((1,), (1,)), ((), ())), preferred_element_type=jnp.float32)
    if masked is not None:
        s = jnp.where(masked, s, LOW)
    top = jnp.max(s, axis=1, keepdims=True)
    width = values.shape[1] // 2
    if first:
        new = jnp.broadcast_to(top, (s.shape[0], width))
    else:
        old = m_ref[rows, :]
        new = jnp.maximum(old, top)
    wide = new if s.shape[1] == width else jnp.concatenate([new] * (s.shape[1] // width), 1)
    p = jnp.exp2(s - wide).astype(jnp.bfloat16)
    pv = jnp.dot(p, values, preferred_element_type=jnp.float32)
    if not first:
        alpha = jnp.exp2(old - new)
        pv = acc_ref[rows, :] * jnp.concatenate([alpha, alpha], 1) + pv
    acc_ref[rows, :] = pv
    m_ref[rows, :] = new


def attend_kernel(
    listed, scale, me_ref, ids, home, q, kv, own, cq, sq, cf, sf, o, lse, qs, acc, m
):
    request = pl.program_id(0)
    stored, groups, span, both = kv.shape
    width = both // 2
    length = q.shape[1]
    heads = q.shape[2] // width
    per = heads // groups
    step = min(2, per)
    mine = me_ref[0]
    here = own.shape[0]
    ones = jnp.ones((span, width), jnp.bfloat16)
    for h in range(heads):
        x = q[0, :, h * width : (h + 1) * width].astype(jnp.float32)
        qs[h * length : (h + 1) * length, :] = (
            turn(x, cq[...], sq[...]) * scale
        ).astype(jnp.bfloat16)
    chunk = step * length

    @pl.when(request // here == mine)
    def _():
        r = request - mine * here
        at = lax.broadcasted_iota(jnp.int32, (chunk, length), 0) % length
        causal = at >= lax.broadcasted_iota(jnp.int32, (chunk, length), 1)
        for g in range(groups):
            pair = own[r, g]
            keys = turn(pair[:, :width].astype(jnp.float32), cq[...], sq[...])
            keys = keys.astype(jnp.bfloat16)
            values = jnp.concatenate([pair[:, width:], ones[:length]], 1)
            for i in range(per // step):
                rows = pl.ds((g * per + i * step) * length, chunk)
                fold(qs[rows, :], keys, values, causal, m, acc, rows, True)

    @pl.when(request // here != mine)
    def _():
        m[...] = jnp.full_like(m, LOW)
        acc[...] = jnp.zeros_like(acc)

    def slot(j, carry):
        at = request * listed + j
        row = home[ids[at]]

        @pl.when(row // stored == mine)
        def _():
            local = row - mine * stored
            cosine, sine = cf[pl.ds(at, 1), :], sf[pl.ds(at, 1), :]
            for g in range(groups):
                pair = kv[local, g]
                keys = turn(pair[:, :width].astype(jnp.float32), cosine, sine)
                keys = keys.astype(jnp.bfloat16)
                values = jnp.concatenate([pair[:, width:], ones], 1)
                for i in range(per // step):
                    rows = pl.ds((g * per + i * step) * length, chunk)
                    fold(qs[rows, :], keys, values, None, m, acc, rows, False)

        return carry

    lax.fori_loop(0, listed, slot, 0)
    eye = lax.broadcasted_iota(jnp.int32, (length, width), 0) == lax.broadcasted_iota(
        jnp.int32, (length, width), 1
    )
    for h in range(heads):
        rows = pl.ds(h * length, length)
        total = acc[rows, width:]
        some = total > 0.0
        safe = jnp.where(some, total, 1.0)
        o[0, :, h * width : (h + 1) * width] = (acc[rows, :width] / safe).astype(jnp.bfloat16)
        level = jnp.where(some, m[rows, :] + jnp.log2(safe), LOW)
        lse[0, h : h + 1, :] = jnp.sum(jnp.where(eye, level, 0.0), axis=0, keepdims=True)


def attend(me, ids, home, q, kv, own, cq, sq, cf, sf):
    requests, length, span = q.shape
    groups, both = kv.shape[1], kv.shape[3]
    width = both // 2
    heads = span // width
    whole = lambda a: pl.BlockSpec(a.shape, lambda i: (0,) * a.ndim, pipeline_mode=pl.Buffered(1))
    smem = pl.BlockSpec(memory_space=pltpu.SMEM)
    return pl.pallas_call(
        functools.partial(
            attend_kernel, ids.shape[0] // requests, math.log2(math.e) / math.sqrt(width)
        ),
        grid=(requests,),
        in_specs=[
            smem,
            smem,
            smem,
            pl.BlockSpec((1, length, span), lambda i: (i, 0, 0)),
            whole(kv),
            whole(own),
            whole(cq),
            whole(sq),
            whole(cf),
            whole(sf),
        ],
        out_specs=[
            pl.BlockSpec((1, length, span), lambda i: (i, 0, 0)),
            pl.BlockSpec((1, heads, length), lambda i: (i, 0, 0)),
        ],
        out_shape=[
            jax.ShapeDtypeStruct((requests, length, span), jnp.bfloat16),
            jax.ShapeDtypeStruct((requests, heads, length), jnp.float32),
        ],
        scratch_shapes=[
            pltpu.VMEM((heads * length, width), jnp.bfloat16),
            pltpu.VMEM((heads * length, 2 * width), jnp.float32),
            pltpu.VMEM((heads * length, width), jnp.float32),
        ],
        compiler_params=pltpu.CompilerParams(vmem_limit_bytes=40 * 1024 * 1024),
    )(me, ids, home, q, kv, own, cq, sq, cf, sf)


def merge_kernel(o, lse, out):
    count, _, heads, length = lse.shape
    width = o.shape[3] // heads
    levels = [lse[c, 0] for c in range(count)]
    top = functools.reduce(jnp.maximum, levels)
    shares = [jnp.exp2(level - top) for level in levels]
    total = functools.reduce(jnp.add, shares)
    shares = [share / total for share in shares]
    for h in range(heads):
        at = slice(h * width, (h + 1) * width)
        result = jnp.zeros((length, width), jnp.float32)
        for c in range(count):
            column = jnp.transpose(jnp.broadcast_to(shares[c][h : h + 1, :], (width, length)))
            result += o[c, 0, :, at].astype(jnp.float32) * column
        out[0, :, at] = result.astype(jnp.bfloat16)


def merge(o, lse):
    count, requests, length, span = o.shape
    heads = lse.shape[2]
    return pl.pallas_call(
        merge_kernel,
        grid=(requests,),
        in_specs=[
            pl.BlockSpec((count, 1, length, span), lambda i: (0, i, 0, 0)),
            pl.BlockSpec((count, 1, heads, length), lambda i: (0, i, 0, 0)),
        ],
        out_specs=pl.BlockSpec((1, length, span), lambda i: (i, 0, 0)),
        out_shape=jax.ShapeDtypeStruct((requests, length, span), jnp.bfloat16),
        compiler_params=pltpu.CompilerParams(vmem_limit_bytes=40 * 1024 * 1024),
    )(o, lse)


def local(
    question_q, question_kv, passage_kv, passage_ids, passage_home, passage_offsets, out_weight
):
    caches, tensors = lax.axis_size("cache"), lax.axis_size("tensor")
    me_cache, me_tensor = lax.axis_index("cache"), lax.axis_index("tensor")
    here, length, span = question_q.shape
    width = passage_kv.shape[-1] // 2
    listed = passage_ids.shape[1]
    inverse = frequencies(width)
    lists = jnp.stack([passage_ids.reshape(-1), passage_offsets.reshape(-1)])
    turned = [lists]
    for k in range(1, caches):
        turned.append(
            lax.ppermute(lists, "cache", [(c, (c + k) % caches) for c in range(caches)])
        )
    order = (me_cache - jnp.arange(caches)) % caches
    lists = jnp.take(jnp.stack(turned), order, axis=0)
    ids, offsets = lists[:, 0].reshape(-1), lists[:, 1].reshape(-1)
    q_all = lax.all_gather(question_q, "cache", axis=0, tiled=True)
    cq, sq = tables(listed * passage_kv.shape[2] + jnp.arange(length), inverse)
    cf, sf = tables(offsets, inverse)
    own = jnp.swapaxes(question_kv, 1, 2)
    o, lse = attend(
        me_cache.reshape(1).astype(jnp.int32), ids, passage_home, q_all, passage_kv, own,
        cq, sq, cf, sf,
    )
    o = lax.all_to_all(o, "cache", split_axis=0, concat_axis=0, tiled=True)
    lse = lax.all_to_all(lse, "cache", split_axis=0, concat_axis=0, tiled=True)
    attended = merge(
        o.reshape((caches, here, length, span)), lse.reshape((caches, here) + lse.shape[1:])
    )
    rows = lax.all_gather(attended.reshape(here * length, span), "cache", axis=0, tiled=True)
    partial = jnp.dot(rows, out_weight, preferred_element_type=jnp.float32)
    summed = lax.psum_scatter(
        partial.astype(jnp.bfloat16), "tensor", scatter_dimension=0, tiled=True
    )
    fan = caches // tensors
    tokens = here * length
    columns = out_weight.shape[1]
    blocks = summed.reshape(fan, tokens, columns)
    pieces = []
    for turn_at in range(fan):
        pairs = []
        for c in range(caches):
            for t in range(tensors):
                to = (t * fan + (turn_at + c % fan) % fan, c // fan)
                pairs.append((c * tensors + t, to[0] * tensors + to[1]))
        block = blocks[0]
        if fan > 1:
            block = lax.dynamic_index_in_dim(blocks, (turn_at + me_cache) % fan, 0, False)
        pieces.append(lax.ppermute(block, ("cache", "tensor"), pairs))
    if fan == 1:
        mixed = pieces[0]
    else:
        stacked = jnp.stack(pieces)
        order = (me_cache - jnp.arange(fan)) % fan
        mixed = jnp.take(stacked, order, axis=0)
        mixed = jnp.swapaxes(mixed, 0, 1).reshape(tokens, fan * columns)
    return mixed.reshape(here, length, -1)


def solution(mesh):
    in_specs = (
        P(("groups", "cache"), None, "tensor"),
        P(("groups", "cache"), None, "tensor", None),
        P(("groups", "cache"), "tensor", None, None),
        P(("groups", "cache"), None),
        P("groups"),
        P(("groups", "cache"), None),
        P("tensor", "cache"),
    )
    out_specs = P(("groups", "cache"), None, "tensor")
    return jax.shard_map(local, mesh=mesh, in_specs=in_specs, out_specs=out_specs, check_vma=False)
```
